256 devices in a mesh: dp: 16 (over z, core), context: 4 (over y), tensor: 4 (over x).
Axes of the slice: x: 4, y: 4, z: 8, core: 2. Of those that a mesh axis runs over, the one named last changes fastest.
Arguments:
- queries: bfloat16 [49152, 2048], P(('dp', 'context', 'tensor')), parts along dimension 0, may hold values from -112 to 112
- keys: bfloat16 [49152, 2048], P(('dp', 'context', 'tensor')), parts along dimension 0, may hold values from -4 to 4
- values: bfloat16 [49152, 2048], P(('dp', 'context', 'tensor')), parts along dimension 0, may hold values from -6 to 6
- doc_ids: int32 [49152], P('dp'), parts along dimension 0, may hold values from 0 to 2, never falling along the last dimension, each value on 1 to 1536 neighbouring positions
- span_lo: int32 [96], P('dp'), parts along dimension 0, may hold values from 0 to 3071, as said below
- span_hi: int32 [96], P('dp'), parts along dimension 0, may hold values from 1 to 3072, as said below
Outputs:
- attended: bfloat16 [49152, 2048], P(('dp', 'context', 'tensor')), parts along dimension 0
The draws below stay inside these ranges and needn't reach their ends.
There are 16 independent parts, one for each index of `dp`. The reference program is written for one: setup_inputs(seed, part) draws one part's arguments, and reference() takes and returns one part's arrays. A program takes and returns all parts, laid end to end along the dimension named above; each array names one. Nothing has to cross between parts.
Inputs may be any that keep to these rules, and one draw needn't show every extreme that they name: `span_lo`: spans are disjoint; span s lies within positions s * 512 to (s + 1) * 512 - 1 and is 128 to 256 long. span_hi[s] > span_lo[s] for every span. `doc_ids`: document ids never fall along the slab.
All inputs are finite; a program needn't handle non-finite values.
Results may differ from the reference program's by a relative error of at most 0.0049.
Values may be sent and summed in bfloat16 or wider, within the bound.
A program may use at most 128 MiB of HBM per device.

```python
import math
import jax
import jax.numpy as jnp
import numpy as np
from jax import lax

D_HEAD = 128
HEADS = 16
SLOT = 512
DOCS = 3
SLAB = 3072
SPANS = 6


def shared_keys(key):
    base_key = jax.random.fold_in(key, 3)
    return jnp.clip(jax.random.normal(base_key, (SLAB, HEADS * D_HEAD), jnp.float32), -4.0, 4.0)


def shared_spans(key):
    span_key = jax.random.fold_in(key, 77)
    first_key, second_key = jax.random.split(span_key)
    offsets = jax.random.randint(first_key, (SPANS,), 0, SLOT // 2)
    extents = jax.random.randint(second_key, (SPANS,), SLOT // 4, SLOT // 2 + 1)
    starts = jnp.arange(SPANS, dtype=jnp.int32) * SLOT + offsets.astype(jnp.int32)
    return (starts, starts + extents.astype(jnp.int32))


def draw_keys(key, part):
    base = shared_keys(key)
    return base.astype(jnp.bfloat16)


def draw_queries(key, part):
    key = jax.random.fold_in(key, 5)
    own = jnp.clip(jax.random.normal(key, (SLAB, HEADS * D_HEAD), jnp.float32), -4.0, 4.0)
    return own.astype(jnp.bfloat16)


def draw_span_lo(key, part):
    starts, ends = shared_spans(key)
    return starts


def draw_span_hi(key, part):
    starts, ends = shared_spans(key)
    return ends


def levels(own_key, dims, shards, least, high):
    factor_of = 1.0
    for axis_at, shards_of in shards:
        steps = jax.random.uniform(jax.random.fold_in(jax.random.fold_in(own_key, 6), axis_at), (shards_of,), jnp.float32, least / len(shards), high / len(shards))
        factor_of = factor_of * jnp.repeat(jnp.exp(steps), dims[axis_at] // shards_of).reshape((-1,) + (1,) * (len(dims) - 1 - axis_at))
    return factor_of


def split_up(count, total, most, slope):
    weights = [(1 << 20) // math.isqrt(rank ** slope) + 1 for rank in range(2, count + 1)]
    rest, given = total - most - (count - 1), [1] * (count - 1)
    while rest > 0:
        movable = [i for i in range(count - 1) if given[i] < most]
        whole, budget = sum([weights[i] for i in movable]), rest
        for i in movable:
            more = min(most - given[i], max(1, budget * weights[i] // whole), rest)
            given[i] = given[i] + more
            rest = rest - more
    return np.array([most] + given)


def ragged(key, count, total, reach, lean):
    if count == 2:
        one = jax.random.randint(key, (), max(1, total - reach), min(reach, total - 1) + 1)
        return jnp.stack([one, total - one])
    sizes = jnp.asarray(split_up(count, total, reach, lean), jnp.int32)
    couples = (count - 1) // 2
    source_of, receiver = sizes[1:1 + 2 * couples:2], sizes[2:2 + 2 * couples:2]
    margin = jnp.minimum(source_of - 1, reach - receiver)
    passed = jax.random.randint(jax.random.fold_in(key, 1), (couples,), 0, 1 << 20) % (margin + 1)
    sizes = sizes.at[1:1 + 2 * couples:2].set(source_of - passed).at[2:2 + 2 * couples:2].set(receiver + passed)
    return sizes[jax.random.permutation(jax.random.fold_in(key, 2), count)]


def scatter_about(key, dims, deviation, limit, cuts=(), kind=jnp.bfloat16):
    values = jax.random.normal(key, dims, jnp.float32) * deviation
    if len(cuts) > 0:
        values = levels(key, dims, cuts, -0.22, 0.18) * values
    return jnp.clip(values, min=-limit, max=limit).astype(kind)


def setup_inputs(seed: int = 0, part: int = 0) -> dict:
    splits = jax.random.split(jax.random.key(seed), 7)
    part_keys = jax.random.split(jax.random.fold_in(splits[6], part), 7)
    return {
        "queries": draw_queries(jax.random.fold_in(jax.random.fold_in(splits[6], part), 71), part),
        "keys": draw_keys(jax.random.fold_in(jax.random.fold_in(splits[6], part), 71), part),
        "values": scatter_about(part_keys[2], (SLAB, HEADS * D_HEAD), 1.0, 6.0, ((0, 16),)),
        "doc_ids": jnp.searchsorted(jnp.cumsum(ragged(part_keys[3], DOCS, SLAB, SLAB // 2, 0)), jnp.arange(SLAB), side="right").astype(jnp.int32),
        "span_lo": draw_span_lo(jax.random.fold_in(jax.random.fold_in(splits[6], part), 71), part),
        "span_hi": draw_span_hi(jax.random.fold_in(jax.random.fold_in(splits[6], part), 71), part),
    }


def span_info(span_lo, span_hi, positions):
    inside = (positions[:, None] >= span_lo[None, :]) & (positions[:, None] < span_hi[None, :])
    number = jnp.arange(span_lo.shape[0], dtype=jnp.int32)[None, :] + 1
    image = jnp.sum(jnp.where(inside, number, 0), axis=1).astype(jnp.int32) - 1
    return image


def reference(queries, keys, values, doc_ids, span_lo, span_hi):
    positions = jnp.arange(SLAB, dtype=jnp.int32)
    image = span_info(span_lo, span_hi, positions)
    allowed = (doc_ids[:, None] == doc_ids[None, :]) & (
        (positions[None, :] <= positions[:, None]) | ((image[:, None] == image[None, :]) & (image[:, None] >= 0)))
    scale = 1.0 / (D_HEAD ** 0.5)
    qsplit = queries.reshape(SLAB, HEADS, D_HEAD).transpose(1, 0, 2)
    ksplit = keys.reshape(SLAB, HEADS, D_HEAD).transpose(1, 0, 2)
    vsplit = values.reshape(SLAB, HEADS, D_HEAD).transpose(1, 0, 2)

    def one_head(triple):
        qhead, khead, vhead = triple
        scores = jnp.dot(qhead, khead.T, preferred_element_type=jnp.float32) * scale
        scores = jnp.where(allowed, scores, -1e30)
        top = jnp.max(scores, axis=1, keepdims=True)
        weights = jnp.where(allowed, jnp.exp(scores - top), 0.0)
        total = jnp.sum(weights, axis=1, keepdims=True)
        summed = jnp.dot(weights.astype(jnp.bfloat16), vhead, preferred_element_type=jnp.float32)
        return summed / total

    result = lax.map(one_head, (qsplit, ksplit, vsplit))
    return result.transpose(1, 0, 2).reshape(SLAB, HEADS * D_HEAD).astype(jnp.bfloat16)
```

```python
import functools

import jax
import jax.numpy as jnp
from jax import lax
from jax.experimental import pallas as pl
from jax.experimental.pallas import tpu as pltpu
from jax.sharding import PartitionSpec as P

MESH = pl.DeviceIdType.MESH
D = 128
LOG2E = 1.4426950408889634
BLOCK = 256
BACK = 64
REACH = 6
FAR = float(2**20)


def kernel(
    nc, nt, q_hbm, k_hbm, v_hbm, docs_hbm, lo_hbm, hi_hbm, out,
    qb, kb, vb, rb, ob, sb, docs, lo, hi, ssem, rsem, osend, orecv, lsem,
):
    rows = q_hbm.shape[0]
    n = nc * nt
    slab = n * rows
    front = kb.shape[0] - slab - 256
    c, t = lax.axis_index("context"), lax.axis_index("tensor")
    me = c * nt + t

    def device(rank):
        return {"context": rank // nt, "tensor": rank % nt}

    def ahead(i):
        return ((c + i // nt) % nc) * nt + (t + i % nt) % nt

    def behind(i):
        return ((c + nc - i // nt) % nc) * nt + (t + nt - i % nt) % nt

    barrier = pltpu.get_barrier_semaphore()
    for i in range(1, n):
        pl.semaphore_signal(barrier, inc=1, device_id=device(ahead(i)), device_id_type=MESH)
    pl.semaphore_wait(barrier, n - 1)

    sources = (k_hbm, v_hbm, q_hbm)
    buffers = (kb, vb, qb)
    offsets = (front, front, 0)

    def columns(rank):
        return pl.ds(pl.multiple_of(rank * D, D), D)

    def place(a, rank):
        return buffers[a].at[pl.ds(pl.multiple_of(offsets[a] + rank * rows, 64), rows), pl.ds(0, D)]

    def send(a, i):
        to = ahead(i)
        return pltpu.make_async_remote_copy(
            src_ref=sources[a].at[:, columns(to)],
            dst_ref=place(a, me),
            send_sem=ssem.at[a, i],
            recv_sem=rsem.at[a, i],
            device_id=device(to),
            device_id_type=MESH,
        )

    def own(a):
        return pltpu.make_async_copy(sources[a].at[:, columns(me)], place(a, me), lsem.at[a])

    small = [
        pltpu.make_async_copy(docs_hbm, docs, lsem.at[3]),
        pltpu.make_async_copy(lo_hbm, lo, lsem.at[4]),
        pltpu.make_async_copy(hi_hbm, hi, lsem.at[5]),
    ]
    for a in range(3):
        for i in range(1, n):
            send(a, i).start()
        own(a).start()
        if a == 0:
            for copy in small:
                copy.start()
    for copy in small:
        copy.wait()

    lane = lax.broadcasted_iota(jnp.int32, (D, D), 1)
    row = lax.broadcasted_iota(jnp.int32, (D, D), 0)
    for b in range(slab // D):
        doc = jnp.transpose(jnp.broadcast_to(docs[b : b + 1, :], (D, D)))
        same = doc == lane
        kb[front + b * D : front + (b + 1) * D, D:] = jnp.where(same, 1.0, 0.0).astype(jnp.bfloat16)
        qb[b * D : (b + 1) * D, D:] = jnp.where(same | (lane > 2), 0.0, -FAR).astype(jnp.bfloat16)
        at = row + b * D
        last = at
        for s in range(lo_hbm.shape[0]):
            last = jnp.where((at >= lo[s]) & (at < hi[s]), hi[s] - 1, last)
        rb[b * D : (b + 1) * D, :] = last
    for start, count in ((0, front), (front + slab, 256)):
        kb[start : start + count, :D] = jnp.zeros((count, D), jnp.bfloat16)
        kb[start : start + count, D:] = jnp.ones((count, D), jnp.bfloat16)
        vb[start : start + count, :D] = jnp.zeros((count, D), jnp.bfloat16)
    vb[:, D:] = jnp.ones((vb.shape[0], D), jnp.bfloat16)

    for a in range(2):
        own(a).wait()
        for i in range(1, n):
            send(a, i).wait_recv()
    own(2).wait()

    factor = LOG2E / D**0.5

    def answer(i, rank):
        return pltpu.make_async_remote_copy(
            src_ref=ob.at[pl.ds(pl.multiple_of(rank * rows, 64), rows), :],
            dst_ref=out.at[:, columns(me)],
            send_sem=osend.at[i],
            recv_sem=orecv.at[i],
            device_id=device(rank),
            device_id_type=MESH,
        )

    def keep():
        return pltpu.make_async_copy(
            ob.at[pl.ds(pl.multiple_of(me * rows, 64), rows), :], out.at[:, columns(me)], lsem.at[6]
        )

    def chunk(i, carry):
        @pl.when(i > 0)
        def _():
            send(2, i).wait_recv()

        rank = behind(i)
        q0 = pl.multiple_of(rank * rows, 64)
        count = jnp.minimum((3 * rank + 2) // 4, REACH)
        base = front + q0 - BACK - BLOCK * count
        qa = qb[pl.ds(q0, rows), :]

        def score(j):
            kj = kb[pl.ds(pl.multiple_of(base + BLOCK * j, 64), BLOCK), :]
            return lax.dot_general(qa, kj, (((1,), (1,)), ((), ())), preferred_element_type=jnp.float32)

        def first(j, top):
            x = score(j)
            sb[j] = x
            return jnp.maximum(top, jnp.maximum(x[:, :D], x[:, D:]))

        top = lax.fori_loop(0, count, first, jnp.full((rows, D), -3e38, jnp.float32))
        limit = rb[pl.ds(q0, rows), :] - (q0 - BACK)
        column = lax.broadcasted_iota(jnp.int32, (rows, D), 1)
        for part in range(2):
            x = score(count + part)
            for half in range(2):
                xh = x[:, half * D : (half + 1) * D]
                xh = jnp.where(column + (part * BLOCK + half * D) <= limit, xh, -1e30)
                sb[count + part, :, half * D : (half + 1) * D] = xh
                top = jnp.maximum(top, xh)
        top = jnp.max(top, axis=1, keepdims=True)

        def second(j, total):
            p = jnp.exp2((sb[j] - top) * factor).astype(jnp.bfloat16)
            vj = vb[pl.ds(pl.multiple_of(base + BLOCK * j, 64), BLOCK), :]
            return total + jnp.dot(p, vj, preferred_element_type=jnp.float32)

        total = lax.fori_loop(0, count + 2, second, jnp.zeros((rows, 2 * D), jnp.float32))
        ob[pl.ds(q0, rows), :] = (total[:, :D] / total[:, D:]).astype(jnp.bfloat16)

        @pl.when(i > 0)
        def _():
            answer(i, rank).start()

        @pl.when(i == 0)
        def _():
            keep().start()

        return carry

    lax.fori_loop(0, n, chunk, 0)

    keep().wait()
    for i in range(1, n):
        answer(i, behind(i)).wait_recv()
    for i in range(1, n):
        answer(i, behind(i)).wait_send()
    for a in range(3):
        for i in range(1, n):
            send(a, i).wait_send()


def solution(mesh):
    nc, nt = mesh.shape["context"], mesh.shape["tensor"]
    n = nc * nt

    def step(queries, keys, values, doc_ids, span_lo, span_hi):
        rows, width = queries.shape
        slab = doc_ids.shape[0]
        spans = span_lo.shape[0]
        padded = 192 + slab + 256
        bf16, f32, i32 = jnp.bfloat16, jnp.float32, jnp.int32
        return pl.pallas_call(
            functools.partial(kernel, nc, nt),
            out_shape=jax.ShapeDtypeStruct((rows, width), bf16),
            in_specs=[pl.BlockSpec(memory_space=pltpu.HBM)] * 6,
            out_specs=pl.BlockSpec(memory_space=pltpu.HBM),
            scratch_shapes=[
                pltpu.VMEM((slab, 2 * D), bf16),
                pltpu.VMEM((padded, 2 * D), bf16),
                pltpu.VMEM((padded, 2 * D), bf16),
                pltpu.VMEM((slab, D), i32),
                pltpu.VMEM((slab, D), bf16),
                pltpu.VMEM((REACH + 2, rows, BLOCK), f32),
                pltpu.VMEM((slab // D, D), i32),
                pltpu.SMEM((spans,), i32),
                pltpu.SMEM((spans,), i32),
                pltpu.SemaphoreType.DMA((3, n)),
                pltpu.SemaphoreType.DMA((3, n)),
                pltpu.SemaphoreType.DMA((n,)),
                pltpu.SemaphoreType.DMA((n,)),
                pltpu.SemaphoreType.DMA((7,)),
            ],
            compiler_params=pltpu.CompilerParams(
                collective_id=0, has_side_effects=True, vmem_limit_bytes=63 << 20
            ),
        )(queries, keys, values, doc_ids.reshape(slab // D, D), span_lo, span_hi)

    rows = P(("dp", "context", "tensor"), None)
    return jax.shard_map(
        step,
        mesh=mesh,
        in_specs=(rows, rows, rows, P("dp"), P("dp"), P("dp")),
        out_specs=rows,
        check_vma=False,
    )
```

```python
import functools

import jax
import jax.numpy as jnp
from jax import lax
from jax.experimental import pallas as pl
from jax.experimental.pallas import tpu as pltpu
from jax.sharding import PartitionSpec as P

MESH = pl.DeviceIdType.MESH
D = 128
LOG2E = 1.4426950408889634
BLOCK = 256
BACK = 64
REACH = 6
FAR = float(2**20)


def kernel(
    nc, nt, q_hbm, k_hbm, v_hbm, docs_hbm, lo_hbm, hi_hbm, out,
    qb, kb, vb, rb, ob, sa, sb, tops, docs, lo, hi, ssem, rsem, osend, orecv, lsem,
):
    rows = q_hbm.shape[0]
    n = nc * nt
    slab = n * rows
    front = BACK + BLOCK * REACH
    c, t = lax.axis_index("context"), lax.axis_index("tensor")
    me = c * nt + t

    def device(rank):
        return {"context": rank // nt, "tensor": rank % nt}

    def ahead(i):
        return ((c + i // nt) % nc) * nt + (t + i % nt) % nt

    def behind(i):
        return ((c + nc - i // nt) % nc) * nt + (t + nt - i % nt) % nt

    barrier = pltpu.get_barrier_semaphore()
    for i in range(1, n):
        pl.semaphore_signal(barrier, inc=1, device_id=device(ahead(i)), device_id_type=MESH)
    pl.semaphore_wait(barrier, n - 1)

    sources = (k_hbm, v_hbm, q_hbm)
    buffers = (kb, vb, qb)
    offsets = (front, front, 0)

    def columns(rank):
        return pl.ds(pl.multiple_of(rank * D, D), D)

    def place(a, rank):
        return buffers[a].at[pl.ds(pl.multiple_of(offsets[a] + rank * rows, 64), rows), pl.ds(0, D)]

    def send(a, i):
        to = ahead(i)
        return pltpu.make_async_remote_copy(
            src_ref=sources[a].at[:, columns(to)],
            dst_ref=place(a, me),
            send_sem=ssem.at[a, i],
            recv_sem=rsem.at[a, i],
            device_id=device(to),
            device_id_type=MESH,
        )

    def own(a):
        return pltpu.make_async_copy(sources[a].at[:, columns(me)], place(a, me), lsem.at[a])

    small = [
        pltpu.make_async_copy(docs_hbm, docs, lsem.at[3]),
        pltpu.make_async_copy(lo_hbm, lo, lsem.at[4]),
        pltpu.make_async_copy(hi_hbm, hi, lsem.at[5]),
    ]
    for a in range(3):
        for i in range(1, n):
            send(a, i).start()
        own(a).start()
        if a == 0:
            for copy in small:
                copy.start()
    for copy in small:
        copy.wait()

    lane = lax.broadcasted_iota(jnp.int32, (D, D), 1)
    row = lax.broadcasted_iota(jnp.int32, (D, D), 0)
    for b in range(slab // D):
        doc = jnp.transpose(jnp.broadcast_to(docs[b : b + 1, :], (D, D)))
        same = doc == lane
        kb[front + b * D : front + (b + 1) * D, D:] = jnp.where(same, 1.0, 0.0).astype(jnp.bfloat16)
        qb[b * D : (b + 1) * D, D:] = jnp.where(same | (lane > 2), 0.0, -FAR).astype(jnp.bfloat16)
        at = row + b * D
        last = at
        for s in range(lo_hbm.shape[0]):
            last = jnp.where((at >= lo[s]) & (at < hi[s]), hi[s] - 1, last)
        rb[b * D : (b + 1) * D, :] = last
    for start, count in ((0, front), (front + slab, BLOCK)):
        kb[start : start + count, :D] = jnp.zeros((count, D), jnp.bfloat16)
        kb[start : start + count, D:] = jnp.ones((count, D), jnp.bfloat16)
        vb[start : start + count, :D] = jnp.zeros((count, D), jnp.bfloat16)
    vb[:, D:] = jnp.ones((vb.shape[0], D), jnp.bfloat16)

    for a in range(2):
        own(a).wait()
        for i in range(1, n):
            send(a, i).wait_recv()
    own(2).wait()

    factor = LOG2E / D**0.5

    def answer(i, rank):
        return pltpu.make_async_remote_copy(
            src_ref=ob.at[pl.ds(pl.multiple_of(rank * rows, 64), rows), :],
            dst_ref=out.at[:, columns(me)],
            send_sem=osend.at[i],
            recv_sem=orecv.at[i],
            device_id=device(rank),
            device_id_type=MESH,
        )

    def keep():
        return pltpu.make_async_copy(
            ob.at[pl.ds(pl.multiple_of(me * rows, 64), rows), :], out.at[:, columns(me)], lsem.at[6]
        )

    column = lax.broadcasted_iota(jnp.int32, (rows, D), 1)

    def key_rows(rank, j):
        start = front + rank * rows - BACK + BLOCK * (j - REACH)
        return pl.ds(pl.multiple_of(start, 64), BLOCK)

    def query_rows(rank):
        return pl.ds(pl.multiple_of(rank * rows, 64), rows)

    def first(rank, scores, top_at):
        qa = qb[query_rows(rank), :]
        limit = rb[query_rows(rank), :] - (rank * rows - BACK)
        top = None
        for j in range(REACH + 2):
            x = lax.dot_general(
                qa, kb[key_rows(rank, j), :], (((1,), (1,)), ((), ())), preferred_element_type=jnp.float32
            )
            left, right = x[:, :D], x[:, D:]
            if j >= REACH:
                offset = (j - REACH) * BLOCK
                left = jnp.where(column + offset <= limit, left, -1e30)
                right = jnp.where(column + (offset + D) <= limit, right, -1e30)
            scores[j, :, :D] = left
            scores[j, :, D:] = right
            larger = jnp.maximum(left, right)
            top = larger if top is None else jnp.maximum(top, larger)
        tops[top_at] = jnp.broadcast_to(jnp.max(top, axis=1, keepdims=True), (rows, D))

    def second(rank, scores, top_at):
        top = tops[top_at][:, :1]
        total = jnp.zeros((rows, 2 * D), jnp.float32)
        for j in range(REACH + 2):
            p = jnp.exp2((scores[j] - top) * factor).astype(jnp.bfloat16)
            total = total + jnp.dot(p, vb[key_rows(rank, j), :], preferred_element_type=jnp.float32)
        ob[query_rows(rank), :] = (total[:, :D] / total[:, D:]).astype(jnp.bfloat16)

    first(me, sa, 0)

    def both(i, held, other, at):
        send(2, i + 1).wait_recv()
        first(behind(i + 1), other, 1 - at)
        second(behind(i), held, at)

    def pair(h, carry):
        both(2 * h, sa, sb, 0)

        @pl.when(h > 0)
        def _():
            answer(2 * h, behind(2 * h)).start()

        @pl.when(h == 0)
        def _():
            keep().start()

        both(2 * h + 1, sb, sa, 1)
        answer(2 * h + 1, behind(2 * h + 1)).start()
        return carry

    lax.fori_loop(0, n // 2 - 1, pair, 0)
    both(n - 2, sa, sb, 0)
    answer(n - 2, behind(n - 2)).start()
    second(behind(n - 1), sb, 1)
    answer(n - 1, behind(n - 1)).start()

    keep().wait()
    for i in range(1, n):
        answer(i, behind(i)).wait_recv()
    for i in range(1, n):
        answer(i, behind(i)).wait_send()
    for a in range(3):
        for i in range(1, n):
            send(a, i).wait_send()


def solution(mesh):
    nc, nt = mesh.shape["context"], mesh.shape["tensor"]
    n = nc * nt

    def step(queries, keys, values, doc_ids, span_lo, span_hi):
        rows, width = queries.shape
        slab = doc_ids.shape[0]
        spans = span_lo.shape[0]
        padded = BACK + BLOCK * REACH + slab + BLOCK
        bf16, f32, i32 = jnp.bfloat16, jnp.float32, jnp.int32
        return pl.pallas_call(
            functools.partial(kernel, nc, nt),
            out_shape=jax.ShapeDtypeStruct((rows, width), bf16),
            in_specs=[pl.BlockSpec(memory_space=pltpu.HBM)] * 6,
            out_specs=pl.BlockSpec(memory_space=pltpu.HBM),
            scratch_shapes=[
                pltpu.VMEM((slab, 2 * D), bf16),
                pltpu.VMEM((padded, 2 * D), bf16),
                pltpu.VMEM((padded, 2 * D), bf16),
                pltpu.VMEM((slab, D), i32),
                pltpu.VMEM((slab, D), bf16),
                pltpu.VMEM((REACH + 2, rows, BLOCK), f32),
                pltpu.VMEM((REACH + 2, rows, BLOCK), f32),
                pltpu.VMEM((2, rows, D), f32),
                pltpu.VMEM((slab // D, D), i32),
                pltpu.SMEM((spans,), i32),
                pltpu.SMEM((spans,), i32),
                pltpu.SemaphoreType.DMA((3, n)),
                pltpu.SemaphoreType.DMA((3, n)),
                pltpu.SemaphoreType.DMA((n,)),
                pltpu.SemaphoreType.DMA((n,)),
                pltpu.SemaphoreType.DMA((7,)),
            ],
            compiler_params=pltpu.CompilerParams(
                collective_id=0, has_side_effects=True, vmem_limit_bytes=63 << 20
            ),
        )(queries, keys, values, doc_ids.reshape(slab // D, D), span_lo, span_hi)

    rows = P(("dp", "context", "tensor"), None)
    return jax.shard_map(
        step,
        mesh=mesh,
        in_specs=(rows, rows, rows, P("dp"), P("dp"), P("dp")),
        out_specs=rows,
        check_vma=False,
    )
```

```python
import functools

import jax
import jax.numpy as jnp
from jax import lax
from jax.experimental import pallas as pl
from jax.experimental.pallas import tpu as pltpu
from jax.sharding import PartitionSpec as P

MESH = pl.DeviceIdType.MESH
D = 128
LOG2E = 1.4426950408889634
BLOCK = 256
BACK = 64
REACH = 6
FAR = float(2**20)


ORDER = [i * 3 % 16 for i in range(16)]

def kernel(
    nc, nt, q_hbm, k_hbm, v_hbm, docs_hbm, lo_hbm, hi_hbm, out,
    qb, kb, vb, rb, ob, sa, sb, tops, docs, lo, hi, ssem, rsem, osend, orecv, lsem,
):
    rows = q_hbm.shape[0]
    n = nc * nt
    slab = n * rows
    front = BACK + BLOCK * REACH
    c, t = lax.axis_index("context"), lax.axis_index("tensor")
    me = c * nt + t

    def device(rank):
        return {"context": rank // nt, "tensor": rank % nt}

    def offset(i):
        if isinstance(i, int):
            return ORDER[i]
        return sum(jnp.where(i == k, ORDER[k], 0) for k in range(n))

    def ahead(i):
        i = offset(i)
        return ((c + i // nt) % nc) * nt + (t + i % nt) % nt

    def behind(i):
        i = offset(i)
        return ((c + nc - i // nt) % nc) * nt + (t + nt - i % nt) % nt

    barrier = pltpu.get_barrier_semaphore()
    for i in range(1, n):
        pl.semaphore_signal(barrier, inc=1, device_id=device(ahead(i)), device_id_type=MESH)
    pl.semaphore_wait(barrier, n - 1)

    sources = (k_hbm, v_hbm, q_hbm)
    buffers = (kb, vb, qb)
    offsets = (front, front, 0)

    def columns(rank):
        return pl.ds(pl.multiple_of(rank * D, D), D)

    def place(a, rank):
        return buffers[a].at[pl.ds(pl.multiple_of(offsets[a] + rank * rows, 64), rows), pl.ds(0, D)]

    def send(a, i):
        to = ahead(i)
        return pltpu.make_async_remote_copy(
            src_ref=sources[a].at[:, columns(to)],
            dst_ref=place(a, me),
            send_sem=ssem.at[a, i],
            recv_sem=rsem.at[a, i],
            device_id=device(to),
            device_id_type=MESH,
        )

    def own(a):
        return pltpu.make_async_copy(sources[a].at[:, columns(me)], place(a, me), lsem.at[a])

    small = [
        pltpu.make_async_copy(docs_hbm, docs, lsem.at[3]),
        pltpu.make_async_copy(lo_hbm, lo, lsem.at[4]),
        pltpu.make_async_copy(hi_hbm, hi, lsem.at[5]),
    ]
    for i in range(1, n):
        send(0, i).start()
    for copy in small + [own(a) for a in range(3)]:
        copy.start()
    for a in (1, 2):
        for i in range(1, n):
            send(a, i).start()
    for copy in small:
        copy.wait()

    lane = lax.broadcasted_iota(jnp.int32, (D, D), 1)
    row = lax.broadcasted_iota(jnp.int32, (D, D), 0)
    for b in range(slab // D):
        doc = jnp.transpose(jnp.broadcast_to(docs[b : b + 1, :], (D, D)))
        same = doc == lane
        kb[front + b * D : front + (b + 1) * D, D:] = jnp.where(same, 1.0, 0.0).astype(jnp.bfloat16)
        qb[b * D : (b + 1) * D, D:] = jnp.where(same | (lane > 2), 0.0, -FAR).astype(jnp.bfloat16)
        at = row + b * D
        last = at
        for s in range(lo_hbm.shape[0]):
            last = jnp.where((at >= lo[s]) & (at < hi[s]), hi[s] - 1, last)
        rb[b * D : (b + 1) * D, :] = last
    for start, count in ((0, front), (front + slab, BLOCK)):
        kb[start : start + count, :D] = jnp.zeros((count, D), jnp.bfloat16)
        kb[start : start + count, D:] = jnp.ones((count, D), jnp.bfloat16)
        vb[start : start + count, :D] = jnp.zeros((count, D), jnp.bfloat16)
    vb[:, D:] = jnp.ones((vb.shape[0], D), jnp.bfloat16)

    def arrive(a):
        own(a).wait()
        for i in range(1, n):
            send(a, i).wait_recv()

    arrive(0)
    own(2).wait()

    factor = LOG2E / D**0.5

    def answer(i, rank):
        return pltpu.make_async_remote_copy(
            src_ref=ob.at[pl.ds(pl.multiple_of(rank * rows, 64), rows), :],
            dst_ref=out.at[:, columns(me)],
            send_sem=osend.at[i],
            recv_sem=orecv.at[i],
            device_id=device(rank),
            device_id_type=MESH,
        )

    def keep():
        return pltpu.make_async_copy(
            ob.at[pl.ds(pl.multiple_of(me * rows, 64), rows), :], out.at[:, columns(me)], lsem.at[6]
        )

    column = lax.broadcasted_iota(jnp.int32, (rows, D), 1)

    def key_rows(rank, j):
        start = front + rank * rows - BACK + BLOCK * (j - REACH)
        return pl.ds(pl.multiple_of(start, 64), BLOCK)

    def query_rows(rank):
        return pl.ds(pl.multiple_of(rank * rows, 64), rows)

    def first(rank, scores, top_at):
        qa = qb[query_rows(rank), :]
        limit = rb[query_rows(rank), :] - (rank * rows - BACK)
        top = None
        for j in range(REACH + 2):
            x = lax.dot_general(
                qa, kb[key_rows(rank, j), :], (((1,), (1,)), ((), ())), preferred_element_type=jnp.float32
            )
            left, right = x[:, :D], x[:, D:]
            if j >= REACH:
                offset = (j - REACH) * BLOCK
                left = jnp.where(column + offset <= limit, left, -1e30)
                right = jnp.where(column + (offset + D) <= limit, right, -1e30)
            scores[j, :, :D] = left
            scores[j, :, D:] = right
            larger = jnp.maximum(left, right)
            top = larger if top is None else jnp.maximum(top, larger)
        tops[top_at] = jnp.broadcast_to(jnp.max(top, axis=1, keepdims=True), (rows, D))

    def second(rank, scores, top_at):
        top = tops[top_at][:, :1]
        total = jnp.zeros((rows, 2 * D), jnp.float32)
        for j in range(REACH + 2):
            p = jnp.exp2((scores[j] - top) * factor).astype(jnp.bfloat16)
            total = total + jnp.dot(p, vb[key_rows(rank, j), :], preferred_element_type=jnp.float32)
        ob[query_rows(rank), :] = (total[:, :D] / total[:, D:]).astype(jnp.bfloat16)

    first(me, sa, 0)
    arrive(1)

    def both(i, held, other, at):
        send(2, i + 1).wait_recv()
        first(behind(i + 1), other, 1 - at)
        second(behind(i), held, at)

    def pair(h, carry):
        both(2 * h, sa, sb, 0)

        @pl.when(h > 0)
        def _():
            answer(2 * h, behind(2 * h)).start()

        @pl.when(h == 0)
        def _():
            keep().start()

        both(2 * h + 1, sb, sa, 1)
        answer(2 * h + 1, behind(2 * h + 1)).start()
        return carry

    lax.fori_loop(0, n // 2 - 1, pair, 0)
    both(n - 2, sa, sb, 0)
    answer(n - 2, behind(n - 2)).start()
    second(behind(n - 1), sb, 1)
    answer(n - 1, behind(n - 1)).start()

    keep().wait()
    for i in range(1, n):
        answer(i, behind(i)).wait_recv()
    for i in range(1, n):
        answer(i, behind(i)).wait_send()
    for a in range(3):
        for i in range(1, n):
            send(a, i).wait_send()


def solution(mesh):
    nc, nt = mesh.shape["context"], mesh.shape["tensor"]
    n = nc * nt

    def step(queries, keys, values, doc_ids, span_lo, span_hi):
        rows, width = queries.shape
        slab = doc_ids.shape[0]
        spans = span_lo.shape[0]
        padded = BACK + BLOCK * REACH + slab + BLOCK
        bf16, f32, i32 = jnp.bfloat16, jnp.float32, jnp.int32
        arrays = (queries, keys, values, doc_ids.reshape(slab // D, D), span_lo, span_hi)
        return pl.pallas_call(
            functools.partial(kernel, nc, nt),
            out_shape=pltpu.VMEM((rows, width), bf16),
            in_specs=[pl.BlockSpec(memory_space=pltpu.HBM)] * 6,
            out_specs=pl.BlockSpec(memory_space=pltpu.VMEM),
            scratch_shapes=[
                pltpu.VMEM((slab, 2 * D), bf16),
                pltpu.VMEM((padded, 2 * D), bf16),
                pltpu.VMEM((padded, 2 * D), bf16),
                pltpu.VMEM((slab, D), i32),
                pltpu.VMEM((slab, D), bf16),
                pltpu.VMEM((REACH + 2, rows, BLOCK), f32),
                pltpu.VMEM((REACH + 2, rows, BLOCK), f32),
                pltpu.VMEM((2, rows, D), f32),
                pltpu.VMEM((slab // D, D), i32),
                pltpu.SMEM((spans,), i32),
                pltpu.SMEM((spans,), i32),
                pltpu.SemaphoreType.DMA((3, n)),
                pltpu.SemaphoreType.DMA((3, n)),
                pltpu.SemaphoreType.DMA((n,)),
                pltpu.SemaphoreType.DMA((n,)),
                pltpu.SemaphoreType.DMA((7,)),
            ],
            compiler_params=pltpu.CompilerParams(
                collective_id=0, has_side_effects=True, vmem_limit_bytes=60 << 20
            ),
        )(*[pltpu.with_memory_space_constraint(x, pltpu.HBM) for x in arrays])

    rows = P(("dp", "context", "tensor"), None)
    return jax.shard_map(
        step,
        mesh=mesh,
        in_specs=(rows, rows, rows, P("dp"), P("dp"), P("dp")),
        out_specs=rows,
        check_vma=False,
    )
```

```python
import functools

import jax
import jax.numpy as jnp
from jax import lax
from jax.experimental import pallas as pl
from jax.experimental.pallas import tpu as pltpu
from jax.sharding import PartitionSpec as P

MESH = pl.DeviceIdType.MESH
D = 128
LOG2E = 1.4426950408889634
BLOCK = 256
BACK = 64
REACH = 6
FAR = float(2**20)


ORDER = (0, 10, 1, 4, 3, 12, 9, 6, 11, 14, 2, 8, 5, 15, 7, 13)

EARLY = 8


def kernel(
    nc, nt, q_hbm, k_hbm, v_hbm, docs_hbm, lo_hbm, hi_hbm, out,
    qb, kb, vb, rb, ob, pb, sa, sb, tops, docs, lo, hi, ssem, rsem, osend, orecv, lsem,
):
    rows = q_hbm.shape[0]
    n = nc * nt
    slab = n * rows
    front = BACK + BLOCK * REACH
    c, t = lax.axis_index("context"), lax.axis_index("tensor")
    me = c * nt + t

    def device(rank):
        return {"context": rank // nt, "tensor": rank % nt}

    def offset(i):
        if isinstance(i, int):
            return ORDER[i]
        return sum(jnp.where(i == k, ORDER[k], 0) for k in range(n))

    def ahead(i):
        i = offset(i)
        return ((c + i // nt) % nc) * nt + (t + i % nt) % nt

    def behind(i):
        i = offset(i)
        return ((c + nc - i // nt) % nc) * nt + (t + nt - i % nt) % nt

    barrier = pltpu.get_barrier_semaphore()
    for i in range(1, n):
        pl.semaphore_signal(barrier, inc=1, device_id=device(ahead(i)), device_id_type=MESH)
    pl.semaphore_wait(barrier, n - 1)

    sources = (k_hbm, q_hbm, v_hbm)
    buffers = (kb, qb, vb)
    offsets = (front, 0, front)

    def columns(rank):
        return pl.ds(pl.multiple_of(rank * D, D), D)

    def place(a, rank):
        return buffers[a].at[pl.ds(pl.multiple_of(offsets[a] + rank * rows, 64), rows), pl.ds(0, D)]

    def send(a, i):
        to = ahead(i)
        return pltpu.make_async_remote_copy(
            src_ref=sources[a].at[:, columns(to)],
            dst_ref=place(a, me),
            send_sem=ssem.at[a, i],
            recv_sem=rsem.at[a, i],
            device_id=device(to),
            device_id_type=MESH,
        )

    def own(a):
        return pltpu.make_async_copy(sources[a].at[:, columns(me)], place(a, me), lsem.at[a])

    small = [
        pltpu.make_async_copy(docs_hbm, docs, lsem.at[3]),
        pltpu.make_async_copy(lo_hbm, lo, lsem.at[4]),
        pltpu.make_async_copy(hi_hbm, hi, lsem.at[5]),
    ]
    for i in range(1, n):
        send(0, i).start()
    for copy in small + [own(a) for a in range(3)]:
        copy.start()
    for i in range(1, EARLY + 1):
        send(1, i).start()
    for i in range(1, n):
        send(2, i).start()
    for i in range(EARLY + 1, n):
        send(1, i).start()
    for copy in small:
        copy.wait()

    lane = lax.broadcasted_iota(jnp.int32, (D, D), 1)
    row = lax.broadcasted_iota(jnp.int32, (D, D), 0)
    for b in range(slab // D):
        doc = jnp.transpose(jnp.broadcast_to(docs[b : b + 1, :], (D, D)))
        same = doc == lane
        kb[front + b * D : front + (b + 1) * D, D:] = jnp.where(same, 1.0, 0.0).astype(jnp.bfloat16)
        qb[b * D : (b + 1) * D, D:] = jnp.where(same | (lane > 2), 0.0, -FAR).astype(jnp.bfloat16)
        at = row + b * D
        last = at
        for s in range(lo_hbm.shape[0]):
            last = jnp.where((at >= lo[s]) & (at < hi[s]), hi[s] - 1, last)
        rb[b * D : (b + 1) * D, :] = last
    for start, count in ((0, front), (front + slab, BLOCK)):
        kb[start : start + count, :D] = jnp.zeros((count, D), jnp.bfloat16)
        kb[start : start + count, D:] = jnp.ones((count, D), jnp.bfloat16)
        vb[start : start + count, :D] = jnp.zeros((count, D), jnp.bfloat16)
    vb[:, D:] = jnp.ones((vb.shape[0], D), jnp.bfloat16)

    def arrive(a):
        own(a).wait()
        for i in range(1, n):
            send(a, i).wait_recv()

    arrive(0)
    own(1).wait()

    factor = LOG2E / D**0.5

    def answer(i, rank):
        return pltpu.make_async_remote_copy(
            src_ref=ob.at[pl.ds(pl.multiple_of(rank * rows, 64), rows), :],
            dst_ref=out.at[:, columns(me)],
            send_sem=osend.at[i],
            recv_sem=orecv.at[i],
            device_id=device(rank),
            device_id_type=MESH,
        )

    def keep():
        return pltpu.make_async_copy(
            ob.at[pl.ds(pl.multiple_of(me * rows, 64), rows), :], out.at[:, columns(me)], lsem.at[6]
        )

    column = lax.broadcasted_iota(jnp.int32, (rows, D), 1)

    def key_rows(rank, j):
        start = front + rank * rows - BACK + BLOCK * (j - REACH)
        return pl.ds(pl.multiple_of(start, 64), BLOCK)

    def query_rows(rank):
        return pl.ds(pl.multiple_of(rank * rows, 64), rows)

    def first(rank, scores, top_at):
        qa = qb[query_rows(rank), :]
        limit = rb[query_rows(rank), :] - (rank * rows - BACK)
        top = None
        for j in range(REACH + 2):
            x = lax.dot_general(
                qa, kb[key_rows(rank, j), :], (((1,), (1,)), ((), ())), preferred_element_type=jnp.float32
            )
            left, right = x[:, :D], x[:, D:]
            if j >= REACH:
                offset = (j - REACH) * BLOCK
                left = jnp.where(column + offset <= limit, left, -1e30)
                right = jnp.where(column + (offset + D) <= limit, right, -1e30)
            scores[j, :, :D] = left
            scores[j, :, D:] = right
            larger = jnp.maximum(left, right)
            top = larger if top is None else jnp.maximum(top, larger)
        tops[top_at] = jnp.broadcast_to(jnp.max(top, axis=1, keepdims=True), (rows, D))

    def second(i, scores, top_at):
        top = tops[top_at][:, :1]
        for j in range(REACH + 2):
            pb[i, :, j * BLOCK : (j + 1) * BLOCK] = jnp.exp2((scores[j] - top) * factor).astype(jnp.bfloat16)

    def third(i):
        rank = behind(i)
        start = pl.multiple_of(front + rank * rows - BACK - BLOCK * REACH, 64)
        total = jnp.dot(
            pb[i], vb[pl.ds(start, (REACH + 2) * BLOCK), :], preferred_element_type=jnp.float32
        )
        ob[query_rows(rank), :] = (total[:, :D] / total[:, D:]).astype(jnp.bfloat16)

    def whole(i, scores, top_at):
        rank = behind(i)
        top = tops[top_at][:, :1]
        total = jnp.zeros((rows, 2 * D), jnp.float32)
        for j in range(REACH + 2):
            p = jnp.exp2((scores[j] - top) * factor).astype(jnp.bfloat16)
            total = total + jnp.dot(p, vb[key_rows(rank, j), :], preferred_element_type=jnp.float32)
        ob[query_rows(rank), :] = (total[:, :D] / total[:, D:]).astype(jnp.bfloat16)

    def reply(i):
        answer(i, behind(i)).start()

    first(me, sa, 0)

    def before(h, carry):
        for e, held, other in ((0, sa, sb), (1, sb, sa)):
            i = 2 * h + e
            send(1, i + 1).wait_recv()
            first(behind(i + 1), other, 1 - e)
            second(i, held, e)
        return carry

    lax.fori_loop(0, EARLY // 2, before, 0)
    second(EARLY, sa, 0)
    arrive(2)

    def product(h, carry):
        third(2 * h + 1)
        third(2 * h + 2)
        reply(2 * h + 1)
        reply(2 * h + 2)
        return carry

    lax.fori_loop(0, EARLY // 2, product, 0)

    send(1, EARLY + 1).wait_recv()
    first(behind(EARLY + 1), sb, 1)
    third(0)
    keep().start()

    def after(h, carry):
        for e, held, other in ((1, sb, sa), (0, sa, sb)):
            i = EARLY + 1 + 2 * h + (1 - e)
            send(1, i + 1).wait_recv()
            first(behind(i + 1), other, 1 - e)
            whole(i, held, e)
            reply(i)
        return carry

    lax.fori_loop(0, (n - 2 - EARLY) // 2, after, 0)
    whole(n - 1, sb, 1)
    reply(n - 1)

    keep().wait()
    for i in range(1, n):
        answer(i, behind(i)).wait_recv()
    for i in range(1, n):
        answer(i, behind(i)).wait_send()
    for a in range(3):
        for i in range(1, n):
            send(a, i).wait_send()


def solution(mesh):
    nc, nt = mesh.shape["context"], mesh.shape["tensor"]
    n = nc * nt

    def step(queries, keys, values, doc_ids, span_lo, span_hi):
        rows, width = queries.shape
        slab = doc_ids.shape[0]
        spans = span_lo.shape[0]
        padded = BACK + BLOCK * REACH + slab + BLOCK
        bf16, f32, i32 = jnp.bfloat16, jnp.float32, jnp.int32
        arrays = (queries, keys, values, doc_ids.reshape(slab // D, D), span_lo, span_hi)
        return pl.pallas_call(
            functools.partial(kernel, nc, nt),
            out_shape=pltpu.VMEM((rows, width), bf16),
            in_specs=[pl.BlockSpec(memory_space=pltpu.HBM)] * 6,
            out_specs=pl.BlockSpec(memory_space=pltpu.VMEM),
            scratch_shapes=[
                pltpu.VMEM((slab, 2 * D), bf16),
                pltpu.VMEM((padded, 2 * D), bf16),
                pltpu.VMEM((padded, 2 * D), bf16),
                pltpu.VMEM((slab, D), i32),
                pltpu.VMEM((slab, D), bf16),
                pltpu.VMEM((n, rows, (REACH + 2) * BLOCK), bf16),
                pltpu.VMEM((REACH + 2, rows, BLOCK), f32),
                pltpu.VMEM((REACH + 2, rows, BLOCK), f32),
                pltpu.VMEM((2, rows, D), f32),
                pltpu.VMEM((slab // D, D), i32),
                pltpu.SMEM((spans,), i32),
                pltpu.SMEM((spans,), i32),
                pltpu.SemaphoreType.DMA((3, n)),
                pltpu.SemaphoreType.DMA((3, n)),
                pltpu.SemaphoreType.DMA((n,)),
                pltpu.SemaphoreType.DMA((n,)),
                pltpu.SemaphoreType.DMA((7,)),
            ],
            compiler_params=pltpu.CompilerParams(
                collective_id=0, has_side_effects=True, vmem_limit_bytes=60 << 20
            ),
        )(*[pltpu.with_memory_space_constraint(x, pltpu.HBM) for x in arrays])

    rows = P(("dp", "context", "tensor"), None)
    return jax.shard_map(
        step,
        mesh=mesh,
        in_specs=(rows, rows, rows, P("dp"), P("dp"), P("dp")),
        out_specs=rows,
        check_vma=False,
    )
```

```python
import functools

import jax
import jax.numpy as jnp
from jax import lax
from jax.experimental import pallas as pl
from jax.experimental.pallas import tpu as pltpu
from jax.sharding import PartitionSpec as P

MESH = pl.DeviceIdType.MESH
D = 128
LOG2E = 1.4426950408889634
BLOCK = 256
BACK = 64
REACH = 6


ORDER = (0, 10, 1, 4, 3, 12, 9, 6, 11, 14, 2, 8, 5, 15, 7, 13)

EARLY = 8


def kernel(
    nc, nt, q_hbm, k_hbm, v_hbm, docs_hbm, lo_hbm, hi_hbm, out,
    qb, kb, vb, rs, rb, ob, pb, sa, sb, tops, docs, lo, hi, ssem, rsem, osend, orecv, lsem,
):
    rows = q_hbm.shape[0]
    n = nc * nt
    slab = n * rows
    front = BACK + BLOCK * REACH
    c, t = lax.axis_index("context"), lax.axis_index("tensor")
    me = c * nt + t
    contexts = [lax.rem(c + d, nc) for d in range(nc)]
    tensors = [lax.rem(t + d, nt) for d in range(nt)]

    def offset(i):
        if isinstance(i, int):
            return ORDER[i]
        return sum(jnp.where(i == k, ORDER[k], 0) for k in range(n))

    def place_of(context, tensor):
        return context * nt + tensor, {"context": context, "tensor": tensor}

    def ahead(i):
        o = offset(i)
        if isinstance(i, int):
            return place_of(contexts[o // nt], tensors[o % nt])
        return place_of(lax.rem(c + lax.div(o, nt), nc), lax.rem(t + lax.rem(o, nt), nt))

    def back(i):
        o = offset(i)
        if isinstance(i, int):
            return place_of(contexts[-(o // nt) % nc], tensors[-(o % nt) % nt])
        return place_of(lax.rem(c + nc - lax.div(o, nt), nc), lax.rem(t + nt - lax.rem(o, nt), nt))

    def behind(i):
        return back(i)[0]

    barrier = pltpu.get_barrier_semaphore()
    for i in range(1, n):
        pl.semaphore_signal(barrier, inc=1, device_id=ahead(i)[1], device_id_type=MESH)
    pl.semaphore_wait(barrier, n - 1)

    sources = (k_hbm, q_hbm, v_hbm)
    buffers = (kb, qb, vb)
    offsets = (front, 0, front)

    def columns(rank):
        return pl.ds(pl.multiple_of(rank * D, D), D)

    def place(a, rank):
        return buffers[a].at[pl.ds(pl.multiple_of(offsets[a] + rank * rows, 64), rows), pl.ds(0, D)]

    def send(a, i):
        to, device = ahead(i)
        return pltpu.make_async_remote_copy(
            src_ref=sources[a].at[:, columns(to)],
            dst_ref=place(a, me),
            send_sem=ssem.at[a, i],
            recv_sem=rsem.at[a, i],
            device_id=device,
            device_id_type=MESH,
        )

    def own(a):
        return pltpu.make_async_copy(sources[a].at[:, columns(me)], place(a, me), lsem.at[a])

    small = [
        pltpu.make_async_copy(docs_hbm, docs, lsem.at[3]),
        pltpu.make_async_copy(lo_hbm, lo, lsem.at[4]),
        pltpu.make_async_copy(hi_hbm, hi, lsem.at[5]),
    ]
    for i in range(1, n):
        send(0, i).start()
    for copy in small + [own(a) for a in range(3)]:
        copy.start()
    for i in range(1, EARLY + 1):
        send(1, i).start()
    for i in range(1, n):
        send(2, i).start()
    for i in range(EARLY + 1, n):
        send(1, i).start()
    for copy in small:
        copy.wait()

    def below(d):
        return jnp.sum(jnp.where(docs[...] < d, 1, 0), axis=(0, 1), keepdims=True)

    second_doc, third_doc = below(1), below(2)
    row = lax.broadcasted_iota(jnp.int32, (D, D), 0)
    for b in range(slab // D):
        doc = jnp.transpose(jnp.broadcast_to(docs[b : b + 1, :], (D, D)))
        at = row + b * D
        last = at
        for s in range(lo_hbm.shape[0]):
            last = jnp.where((at >= lo[s]) & (at < hi[s]), hi[s] - 1, last)
        end = jnp.where(doc == 0, second_doc, jnp.where(doc == 1, third_doc, slab))
        rb[b * D : (b + 1) * D, :] = jnp.minimum(last, end - 1)
        rs[b * D : (b + 1) * D, :] = jnp.where(doc == 0, 0, jnp.where(doc == 1, second_doc, third_doc))
    for start, count in ((0, front), (front + slab, BLOCK)):
        kb[start : start + count, :] = jnp.zeros((count, D), jnp.bfloat16)
        vb[start : start + count, :D] = jnp.zeros((count, D), jnp.bfloat16)
    vb[:, D:] = jnp.ones((vb.shape[0], D), jnp.bfloat16)

    def arrive(a):
        own(a).wait()
        for i in range(1, n):
            send(a, i).wait_recv()

    arrive(0)
    own(1).wait()

    factor = LOG2E / D**0.5

    def answer(i):
        rank, device = back(i)
        return pltpu.make_async_remote_copy(
            src_ref=ob.at[pl.ds(pl.multiple_of(rank * rows, 64), rows), :],
            dst_ref=out.at[:, columns(me)],
            send_sem=osend.at[i],
            recv_sem=orecv.at[i],
            device_id=device,
            device_id_type=MESH,
        )

    def keep():
        return pltpu.make_async_copy(
            ob.at[pl.ds(pl.multiple_of(me * rows, 64), rows), :], out.at[:, columns(me)], lsem.at[6]
        )

    column = lax.broadcasted_iota(jnp.int32, (rows, D), 1)

    def key_rows(rank, j):
        start = front + rank * rows - BACK + BLOCK * (j - REACH)
        return pl.ds(pl.multiple_of(start, 64), BLOCK)

    def query_rows(rank):
        return pl.ds(pl.multiple_of(rank * rows, 64), rows)

    def first(rank, scores, top_at):
        qa = qb[query_rows(rank), :]
        origin = rank * rows - BACK - BLOCK * REACH
        least, limit = rs[query_rows(rank), :] - origin, rb[query_rows(rank), :] - origin
        top = None
        for j in range(REACH + 2):
            x = lax.dot_general(
                qa, kb[key_rows(rank, j), :], (((1,), (1,)), ((), ())), preferred_element_type=jnp.float32
            )
            left, right = x[:, :D], x[:, D:]
            near, far = column + j * BLOCK, column + (j * BLOCK + D)
            left = jnp.where((near >= least) & (near <= limit) if j >= REACH else near >= least, left, -1e30)
            right = jnp.where((far >= least) & (far <= limit) if j >= REACH else far >= least, right, -1e30)
            scores[j, :, :D] = left
            scores[j, :, D:] = right
            larger = jnp.maximum(left, right)
            top = larger if top is None else jnp.maximum(top, larger)
        tops[top_at] = jnp.broadcast_to(jnp.max(top, axis=1, keepdims=True), (rows, D))

    def second(i, scores, top_at):
        top = tops[top_at][:, :1]
        for j in range(REACH + 2):
            pb[i, :, j * BLOCK : (j + 1) * BLOCK] = jnp.exp2((scores[j] - top) * factor).astype(jnp.bfloat16)

    def third(i):
        rank = behind(i)
        start = pl.multiple_of(front + rank * rows - BACK - BLOCK * REACH, 64)
        total = jnp.dot(
            pb[i], vb[pl.ds(start, (REACH + 2) * BLOCK), :], preferred_element_type=jnp.float32
        )
        ob[query_rows(rank), :] = (total[:, :D] / total[:, D:]).astype(jnp.bfloat16)

    def whole(i, scores, top_at):
        rank = behind(i)
        top = tops[top_at][:, :1]
        total = jnp.zeros((rows, 2 * D), jnp.float32)
        for j in range(REACH + 2):
            p = jnp.exp2((scores[j] - top) * factor).astype(jnp.bfloat16)
            total = total + jnp.dot(p, vb[key_rows(rank, j), :], preferred_element_type=jnp.float32)
        ob[query_rows(rank), :] = (total[:, :D] / total[:, D:]).astype(jnp.bfloat16)

    def reply(i):
        answer(i).start()

    first(me, sa, 0)

    def before(h, carry):
        for e, held, other in ((0, sa, sb), (1, sb, sa)):
            i = 2 * h + e
            send(1, i + 1).wait_recv()
            first(behind(i + 1), other, 1 - e)
            second(i, held, e)
        return carry

    lax.fori_loop(0, EARLY // 2, before, 0)
    second(EARLY, sa, 0)
    arrive(2)

    def product(h, carry):
        third(2 * h + 1)
        third(2 * h + 2)
        reply(2 * h + 1)
        reply(2 * h + 2)
        return carry

    lax.fori_loop(0, EARLY // 2, product, 0)

    send(1, EARLY + 1).wait_recv()
    first(behind(EARLY + 1), sb, 1)

    def after(h, carry):
        for e, held, other in ((1, sb, sa), (0, sa, sb)):
            i = EARLY + 1 + 2 * h + (1 - e)
            send(1, i + 1).wait_recv()
            first(behind(i + 1), other, 1 - e)
            whole(i, held, e)
            reply(i)
        return carry

    lax.fori_loop(0, (n - 2 - EARLY) // 2, after, 0)
    whole(n - 1, sb, 1)
    reply(n - 1)
    third(0)
    keep().start()

    keep().wait()
    for a in range(3):
        for i in range(1, n):
            send(a, i).wait_send()
    for i in range(1, n):
        answer(i).wait_send()
    for i in range(1, n):
        answer(i).wait_recv()


def solution(mesh):
    nc, nt = mesh.shape["context"], mesh.shape["tensor"]
    n = nc * nt

    def step(queries, keys, values, doc_ids, span_lo, span_hi):
        rows, width = queries.shape
        slab = doc_ids.shape[0]
        spans = span_lo.shape[0]
        padded = BACK + BLOCK * REACH + slab + BLOCK
        bf16, f32, i32 = jnp.bfloat16, jnp.float32, jnp.int32
        arrays = (queries, keys, values, doc_ids.reshape(slab // D, D), span_lo, span_hi)
        return pl.pallas_call(
            functools.partial(kernel, nc, nt),
            out_shape=pltpu.VMEM((rows, width), bf16),
            in_specs=[pl.BlockSpec(memory_space=pltpu.HBM)] * 6,
            out_specs=pl.BlockSpec(memory_space=pltpu.VMEM),
            scratch_shapes=[
                pltpu.VMEM((slab, D), bf16),
                pltpu.VMEM((padded, D), bf16),
                pltpu.VMEM((padded, 2 * D), bf16),
                pltpu.VMEM((slab, D), i32),
                pltpu.VMEM((slab, D), i32),
                pltpu.VMEM((slab, D), bf16),
                pltpu.VMEM((n, rows, (REACH + 2) * BLOCK), bf16),
                pltpu.VMEM((REACH + 2, rows, BLOCK), f32),
                pltpu.VMEM((REACH + 2, rows, BLOCK), f32),
                pltpu.VMEM((2, rows, D), f32),
                pltpu.VMEM((slab // D, D), i32),
                pltpu.SMEM((spans,), i32),
                pltpu.SMEM((spans,), i32),
                pltpu.SemaphoreType.DMA((3, n)),
                pltpu.SemaphoreType.DMA((3, n)),
                pltpu.SemaphoreType.DMA((n,)),
                pltpu.SemaphoreType.DMA((n,)),
                pltpu.SemaphoreType.DMA((7,)),
            ],
            compiler_params=pltpu.CompilerParams(
                collective_id=0, has_side_effects=True, vmem_limit_bytes=60 << 20
            ),
        )(*[pltpu.with_memory_space_constraint(x, pltpu.HBM) for x in arrays])

    rows = P(("dp", "context", "tensor"), None)
    return jax.shard_map(
        step,
        mesh=mesh,
        in_specs=(rows, rows, rows, P("dp"), P("dp"), P("dp")),
        out_specs=rows,
        check_vma=False,
    )
```

```python
import functools

import jax
import jax.numpy as jnp
from jax import lax
from jax.experimental import pallas as pl
from jax.experimental.pallas import tpu as pltpu
from jax.sharding import PartitionSpec as P

MESH = pl.DeviceIdType.MESH
D = 128
LOG2E = 1.4426950408889634
BLOCK = 256
BACK = 64
REACH = 6


ORDER = (0, 10, 1, 4, 3, 12, 9, 6, 11, 14, 2, 8, 5, 15, 7, 13)

EARLY = 4


def kernel(
    nc, nt, q_hbm, k_hbm, v_hbm, docs_hbm, lo_hbm, hi_hbm, out,
    qb, kb, vb, rs, rb, ob, pb, sa, sb, tops, docs, lo, hi, ssem, rsem, osend, orecv, lsem,
):
    rows = q_hbm.shape[0]
    n = nc * nt
    slab = n * rows
    front = BACK + BLOCK * REACH
    c, t = lax.axis_index("context"), lax.axis_index("tensor")
    me = c * nt + t
    contexts = [lax.rem(c + d, nc) for d in range(nc)]
    tensors = [lax.rem(t + d, nt) for d in range(nt)]

    def offset(i):
        if isinstance(i, int):
            return ORDER[i]
        return sum(jnp.where(i == k, ORDER[k], 0) for k in range(n))

    def place_of(context, tensor):
        return context * nt + tensor, {"context": context, "tensor": tensor}

    def ahead(i):
        o = offset(i)
        if isinstance(i, int):
            return place_of(contexts[o // nt], tensors[o % nt])
        return place_of(lax.rem(c + lax.div(o, nt), nc), lax.rem(t + lax.rem(o, nt), nt))

    def back(i):
        o = offset(i)
        if isinstance(i, int):
            return place_of(contexts[-(o // nt) % nc], tensors[-(o % nt) % nt])
        return place_of(lax.rem(c + nc - lax.div(o, nt), nc), lax.rem(t + nt - lax.rem(o, nt), nt))

    def behind(i):
        return back(i)[0]

    barrier = pltpu.get_barrier_semaphore()
    for i in range(1, n):
        pl.semaphore_signal(barrier, inc=1, device_id=ahead(i)[1], device_id_type=MESH)
    pl.semaphore_wait(barrier, n - 1)

    sources = (k_hbm, q_hbm, v_hbm)
    buffers = (kb, qb, vb)
    offsets = (front, 0, front)

    def columns(rank):
        return pl.ds(pl.multiple_of(rank * D, D), D)

    def place(a, rank):
        return buffers[a].at[pl.ds(pl.multiple_of(offsets[a] + rank * rows, 64), rows), pl.ds(0, D)]

    def send(a, i):
        to, device = ahead(i)
        return pltpu.make_async_remote_copy(
            src_ref=sources[a].at[:, columns(to)],
            dst_ref=place(a, me),
            send_sem=ssem.at[a, i],
            recv_sem=rsem.at[a, i],
            device_id=device,
            device_id_type=MESH,
        )

    def own(a):
        return pltpu.make_async_copy(sources[a].at[:, columns(me)], place(a, me), lsem.at[a])

    small = [
        pltpu.make_async_copy(docs_hbm, docs, lsem.at[3]),
        pltpu.make_async_copy(lo_hbm, lo, lsem.at[4]),
        pltpu.make_async_copy(hi_hbm, hi, lsem.at[5]),
    ]
    for i in range(1, n):
        send(0, i).start()
    for copy in small + [own(a) for a in range(3)]:
        copy.start()
    for i in range(1, EARLY + 1):
        send(1, i).start()
    for i in range(1, n):
        send(2, i).start()
    for i in range(EARLY + 1, n):
        send(1, i).start()
    for copy in small:
        copy.wait()

    def below(d):
        return jnp.sum(jnp.where(docs[...] < d, 1, 0), axis=(0, 1), keepdims=True)

    second_doc, third_doc = below(1), below(2)
    row = lax.broadcasted_iota(jnp.int32, (D, D), 0)
    for b in range(slab // D):
        doc = jnp.transpose(jnp.broadcast_to(docs[b : b + 1, :], (D, D)))
        at = row + b * D
        last = at
        for s in range(lo_hbm.shape[0]):
            last = jnp.where((at >= lo[s]) & (at < hi[s]), hi[s] - 1, last)
        end = jnp.where(doc == 0, second_doc, jnp.where(doc == 1, third_doc, slab))
        rb[b * D : (b + 1) * D, :] = jnp.minimum(last, end - 1)
        rs[b * D : (b + 1) * D, :] = jnp.where(doc == 0, 0, jnp.where(doc == 1, second_doc, third_doc))
    for start, count in ((0, front), (front + slab, BLOCK)):
        kb[start : start + count, :] = jnp.zeros((count, D), jnp.bfloat16)
        vb[start : start + count, :D] = jnp.zeros((count, D), jnp.bfloat16)
    vb[:, D:] = jnp.ones((vb.shape[0], D), jnp.bfloat16)

    def arrive(a):
        own(a).wait()
        for i in range(1, n):
            send(a, i).wait_recv()

    arrive(0)
    own(1).wait()

    factor = LOG2E / D**0.5

    def answer(i):
        rank, device = back(i)
        return pltpu.make_async_remote_copy(
            src_ref=ob.at[pl.ds(pl.multiple_of(rank * rows, 64), rows), :],
            dst_ref=out.at[:, columns(me)],
            send_sem=osend.at[i],
            recv_sem=orecv.at[i],
            device_id=device,
            device_id_type=MESH,
        )

    def keep():
        return pltpu.make_async_copy(
            ob.at[pl.ds(pl.multiple_of(me * rows, 64), rows), :], out.at[:, columns(me)], lsem.at[6]
        )

    column = lax.broadcasted_iota(jnp.int32, (rows, D), 1)

    def key_rows(rank, j):
        start = front + rank * rows - BACK + BLOCK * (j - REACH)
        return pl.ds(pl.multiple_of(start, 64), BLOCK)

    def query_rows(rank):
        return pl.ds(pl.multiple_of(rank * rows, 64), rows)

    def first(rank, scores, top_at):
        qa = qb[query_rows(rank), :]
        origin = rank * rows - BACK - BLOCK * REACH
        least, limit = rs[query_rows(rank), :] - origin, rb[query_rows(rank), :] - origin
        top = None
        for j in range(REACH + 2):
            x = lax.dot_general(
                qa, kb[key_rows(rank, j), :], (((1,), (1,)), ((), ())), preferred_element_type=jnp.float32
            )
            left, right = x[:, :D], x[:, D:]
            near, far = column + j * BLOCK, column + (j * BLOCK + D)
            left = jnp.where((near >= least) & (near <= limit) if j >= REACH else near >= least, left, -1e30)
            right = jnp.where((far >= least) & (far <= limit) if j >= REACH else far >= least, right, -1e30)
            scores[j, :, :D] = left
            scores[j, :, D:] = right
            larger = jnp.maximum(left, right)
            top = larger if top is None else jnp.maximum(top, larger)
        tops[top_at] = jnp.broadcast_to(jnp.max(top, axis=1, keepdims=True), (rows, D))

    def second(i, scores, top_at):
        top = tops[top_at][:, :1]
        for j in range(REACH + 2):
            pb[i, :, j * BLOCK : (j + 1) * BLOCK] = jnp.exp2((scores[j] - top) * factor).astype(jnp.bfloat16)

    def third(i):
        rank = behind(i)
        start = pl.multiple_of(front + rank * rows - BACK - BLOCK * REACH, 64)
        total = jnp.dot(
            pb[i], vb[pl.ds(start, (REACH + 2) * BLOCK), :], preferred_element_type=jnp.float32
        )
        ob[query_rows(rank), :] = (total[:, :D] / total[:, D:]).astype(jnp.bfloat16)

    def whole(i, scores, top_at):
        rank = behind(i)
        top = tops[top_at][:, :1]
        total = jnp.zeros((rows, 2 * D), jnp.float32)
        for j in range(REACH + 2):
            p = jnp.exp2((scores[j] - top) * factor).astype(jnp.bfloat16)
            total = total + jnp.dot(p, vb[key_rows(rank, j), :], preferred_element_type=jnp.float32)
        ob[query_rows(rank), :] = (total[:, :D] / total[:, D:]).astype(jnp.bfloat16)

    def reply(i):
        answer(i).start()

    first(me, sa, 0)

    def before(h, carry):
        for e, held, other in ((0, sa, sb), (1, sb, sa)):
            i = 2 * h + e
            send(1, i + 1).wait_recv()
            first(behind(i + 1), other, 1 - e)
            second(i, held, e)
        return carry

    lax.fori_loop(0, EARLY // 2, before, 0)
    second(EARLY, sa, 0)
    arrive(2)

    def product(h, carry):
        third(2 * h + 1)
        third(2 * h + 2)
        reply(2 * h + 1)
        reply(2 * h + 2)
        return carry

    lax.fori_loop(0, EARLY // 2, product, 0)

    send(1, EARLY + 1).wait_recv()
    first(behind(EARLY + 1), sb, 1)

    def after(h, carry):
        for e, held, other in ((1, sb, sa), (0, sa, sb)):
            i = EARLY + 1 + 2 * h + (1 - e)
            send(1, i + 1).wait_recv()
            first(behind(i + 1), other, 1 - e)
            whole(i, held, e)
            reply(i)
        return carry

    lax.fori_loop(0, (n - 2 - EARLY) // 2, after, 0)
    whole(n - 1, sb, 1)
    reply(n - 1)
    third(0)
    keep().start()

    keep().wait()
    for a in range(3):
        for i in range(1, n):
            send(a, i).wait_send()
    for i in range(1, n):
        answer(i).wait_send()
    for i in range(1, n):
        answer(i).wait_recv()


def solution(mesh):
    nc, nt = mesh.shape["context"], mesh.shape["tensor"]
    n = nc * nt

    def step(queries, keys, values, doc_ids, span_lo, span_hi):
        rows, width = queries.shape
        slab = doc_ids.shape[0]
        spans = span_lo.shape[0]
        padded = BACK + BLOCK * REACH + slab + BLOCK
        bf16, f32, i32 = jnp.bfloat16, jnp.float32, jnp.int32
        arrays = (queries, keys, values, doc_ids.reshape(slab // D, D), span_lo, span_hi)
        return pl.pallas_call(
            functools.partial(kernel, nc, nt),
            out_shape=pltpu.VMEM((rows, width), bf16),
            in_specs=[pl.BlockSpec(memory_space=pltpu.HBM)] * 6,
            out_specs=pl.BlockSpec(memory_space=pltpu.VMEM),
            scratch_shapes=[
                pltpu.VMEM((slab, D), bf16),
                pltpu.VMEM((padded, D), bf16),
                pltpu.VMEM((padded, 2 * D), bf16),
                pltpu.VMEM((slab, D), i32),
                pltpu.VMEM((slab, D), i32),
                pltpu.VMEM((slab, D), bf16),
                pltpu.VMEM((n, rows, (REACH + 2) * BLOCK), bf16),
                pltpu.VMEM((REACH + 2, rows, BLOCK), f32),
                pltpu.VMEM((REACH + 2, rows, BLOCK), f32),
                pltpu.VMEM((2, rows, D), f32),
                pltpu.VMEM((slab // D, D), i32),
                pltpu.SMEM((spans,), i32),
                pltpu.SMEM((spans,), i32),
                pltpu.SemaphoreType.DMA((3, n)),
                pltpu.SemaphoreType.DMA((3, n)),
                pltpu.SemaphoreType.DMA((n,)),
                pltpu.SemaphoreType.DMA((n,)),
                pltpu.SemaphoreType.DMA((7,)),
            ],
            compiler_params=pltpu.CompilerParams(
                collective_id=0, has_side_effects=True, vmem_limit_bytes=60 << 20
            ),
        )(*[pltpu.with_memory_space_constraint(x, pltpu.HBM) for x in arrays])

    rows = P(("dp", "context", "tensor"), None)
    return jax.shard_map(
        step,
        mesh=mesh,
        in_specs=(rows, rows, rows, P("dp"), P("dp"), P("dp")),
        out_specs=rows,
        check_vma=False,
    )
```
